32 devices in a mesh: occ: 4 (over z), vir: 8 (over y, x, core).
Axes of the slice: x: 2, y: 2, z: 4, core: 2. Of those that a mesh axis runs over, the one named last changes fastest.
Arguments:
- amplitudes: float32 [6144, 1024], P('vir', 'occ'), may hold values from -6 to 6
- integrals: float32 [768, 40960], P('occ', 'vir'), may hold values from -0.21875 to 0.21875
- eps_vir: float32 [40960], P('vir'), may hold values from 0.5 to 3
- eps_occ: float32 [1024], P('occ'), may hold values from -2 to -0.5
- panel_owner: int32 [12], replicated, may hold values from 0 to 7
- block_target: int32 [512], replicated, may hold values from 0 to 511, as said below
Outputs:
- ladder_tiles: float32 [40960, 1024], P('vir', 'occ')
The draws below stay inside these ranges and needn't reach their ends.
Inputs may be any that keep to these rules, and one draw needn't show every extreme that they name: block_target is a permutation. The 64 blocks of each index of vir go to 4 owner indices, exactly 16 to each, and each owner receives exactly 16 blocks from each of 4 senders; block b of the whole lies on index b // 64.
All inputs are finite; a program needn't handle non-finite values.
Results may differ from the reference program's by a relative error of at most 0.000082.
Values sent between devices are 32-bit elements; how exact they have to be, the bound alone decides.
No kernel may reach another device: no remote copies, remote signals or barrier semaphores. Data moves between devices by JAX's collectives and lax.ppermute only.
A program may use at most 128 MiB of HBM per device.

```python
import jax
import jax.numpy as jnp
from jax import lax

PANEL = 64
STEPS = 12
VP_DEV = 5120
NB_DEV = 64
SP = 768
VP = 40960
OP = 1024
NBLK = 512
BLK = 80
AROWS = 6144
N_VIR = 8


def draw_block_target(key, part):
    devices = NBLK // NB_DEV
    capacity = max(2, 2 * NB_DEV // devices)
    rounds = NB_DEV // capacity
    key_shift, key_order, key_slot = jax.random.split(key, 3)
    shifts = jax.random.permutation(key_shift, devices)[:rounds]
    orders = jax.vmap(lambda sub_key: jax.random.permutation(sub_key, NB_DEV))(jax.random.split(key_order, devices))
    slotting = jax.vmap(lambda sub_key: jax.random.permutation(sub_key, NB_DEV))(jax.random.split(key_slot, devices))
    round_of = orders // capacity
    within = orders % capacity
    senders = jnp.arange(devices)[:, None]
    owner = (senders + shifts[round_of]) % devices
    slot = slotting[owner, round_of * capacity + within]
    return (owner * NB_DEV + slot).reshape(-1).astype(jnp.int32)


def set_ends(values, own_key, least, top_value):
    dims = values.shape
    index_at = [jax.random.randint(jax.random.fold_in(own_key, axis), (), 0, dims[axis]) for axis in range(len(dims))]
    values = values.at[tuple(index_at)].set(least)
    longest = dims.index(max(dims))
    index_at[longest] = (index_at[longest] + 1) % dims[longest]
    return values.at[tuple(index_at)].set(top_value)


def levels(rng, shape, cuts, least, top_value):
    def one(position, blocks):
        draws = jax.random.uniform(jax.random.fold_in(jax.random.fold_in(rng, 6), position), (blocks,), jnp.float32, least / len(cuts), top_value / len(cuts))
        return jnp.repeat(jnp.exp(draws), shape[position] // blocks).reshape((-1,) + (1,) * (len(shape) - position - 1))

    level = one(*cuts[0])
    for cut in cuts[1:]:
        level = level * one(*cut)
    return level


def normal_values(key, dims, deviation, bound, pieces=(), dtype=jnp.bfloat16):
    entries = deviation * jax.random.normal(key, dims, jnp.float32)
    if pieces:
        entries = entries * levels(key, dims, pieces, -0.22, 0.18)
    return jnp.clip(entries, -bound, bound).astype(dtype)


def setup_inputs(seed: int = 0) -> dict:
    key_of = jax.random.split(jax.random.key(seed), 7)
    return {
        "amplitudes": normal_values(key_of[0], (AROWS, OP), 1.0, 6.0, ((0, 8), (1, 4)), jnp.float32),
        "integrals": normal_values(key_of[1], (SP, VP), SP ** -0.5, 0.21875, ((0, 4), (1, 8)), jnp.float32),
        "eps_vir": jnp.clip(0.5 + 2.5 * jax.random.uniform(key_of[2], (VP,), jnp.float32) ** levels(key_of[2], (VP,), ((0, 8),), -0.2, 0.2), 0.5, 3.0),
        "eps_occ": jnp.clip(-2.0 + 1.5 * jax.random.uniform(key_of[3], (OP,), jnp.float32) ** levels(key_of[3], (OP,), ((0, 4),), -0.2, 0.2), -2.0, -0.5),
        "panel_owner": set_ends(jax.random.randint(key_of[4], (STEPS,), 0, N_VIR), jax.random.fold_in(key_of[4], 1), 0, N_VIR - 1).astype(jnp.int32),
        "block_target": draw_block_target(jax.random.fold_in(key_of[6], 71), 0),
    }


def reference(amplitudes, integrals, eps_vir, eps_occ, panel_owner, block_target):
    picked = []
    for step_index in range(STEPS):
        first_row = ((panel_owner[step_index] * STEPS + step_index) * PANEL).astype(jnp.int32)
        picked.append(lax.dynamic_slice_in_dim(amplitudes, first_row, PANEL, 0))
    panels = jnp.concatenate(picked, 0)
    grouped = integrals.reshape(SP, N_VIR, VP_DEV).transpose(1, 0, 2)
    energies = eps_vir.reshape(N_VIR, VP_DEV)

    def one_group(pair_args):
        group_ints, group_eps = pair_args
        ladder = lax.dot_general(group_ints, panels, (((0,), (0,)), ((), ())),
                                 precision=lax.Precision.HIGHEST, preferred_element_type=jnp.float32)
        return ladder / (group_eps[:, None] - eps_occ[None, :])

    scaled = lax.map(one_group, (grouped, energies))
    blocks = scaled.reshape(NBLK, BLK, OP)
    placed = jnp.zeros_like(blocks).at[block_target].set(blocks)
    return placed.reshape(VP, OP)
```

```python
import functools

import jax
import jax.numpy as jnp
from jax import lax
from jax.experimental import pallas as pl
from jax.experimental.pallas import tpu as pltpu
from jax.sharding import PartitionSpec as P

STEPS = 12
NB_DEV = 64
LANES = 128
CHUNKS = 8
GROUP = 8
VMEM_LIMIT = 48 * 1024 * 1024

f32 = jnp.float32
bf16 = jnp.bfloat16


def params():
    return pltpu.CompilerParams(vmem_limit_bytes=VMEM_LIMIT)


def routing(block_target, device_id, senders, capacity, chunks):
    per_chunk = capacity // chunks
    fanout = NB_DEV // capacity
    in_chunk = fanout * per_chunk
    place = jnp.arange(NB_DEV)
    owners = (block_target // NB_DEV).reshape(senders, NB_DEV)
    same = owners[:, :, None] == owners[:, None, :]
    rank = jnp.sum((same & (place[None, None, :] < place[None, :, None])).astype(jnp.int32), axis=2)

    mine = lax.dynamic_index_in_dim(owners, device_id, 0, keepdims=False)
    my_rank = lax.dynamic_index_in_dim(rank, device_id, 0, keepdims=False)
    ordinal = jnp.sum((mine[None, :] < mine[:, None]).astype(jnp.int32), axis=1) // capacity
    position = (my_rank // per_chunk) * in_chunk + ordinal * per_chunk + my_rank % per_chunk
    order = jnp.sum(jnp.where(position[None, :] == place[:, None], place[None, :], 0), axis=1)

    ids = jnp.arange(senders)
    before = jnp.sum((mine[None, :] < ids[:, None]).astype(jnp.int32), axis=1)
    present = jnp.sum((mine[None, :] == ids[:, None]).astype(jnp.int32), axis=1) > 0
    group_of_owner = jnp.where(present, before // capacity, 0)

    to_me = owners == device_id
    wanted = jnp.where(to_me, block_target.reshape(senders, NB_DEV) % NB_DEV, 0)
    sends = jnp.sum(to_me.astype(jnp.int32), axis=1)
    earlier = jnp.sum(jnp.where(ids[None, :] < ids[:, None], sends[None, :], 0), axis=1) // capacity
    entry = (rank // per_chunk) * in_chunk + earlier[:, None] * per_chunk + rank % per_chunk
    entry = jnp.where(to_me, entry, -1).reshape(-1)
    hit = entry[None, :] == place[:, None]
    slot = (ids[:, None] * per_chunk + rank % per_chunk).reshape(-1)
    source = jnp.sum(jnp.where(hit, slot[None, :], 0), axis=1)
    target = jnp.sum(jnp.where(hit, wanted.reshape(-1)[None, :], 0), axis=1)
    return order, group_of_owner, source, target


def reorder(integrals, order, block_cols):
    rows, cols = integrals.shape
    count = order.shape[0]
    last_tile = cols // LANES - 1

    def first_tile(block):
        return lax.div(block * block_cols, LANES)

    def body(order_ref, *refs):
        out_ref = refs[-1]
        step = pl.program_id(0)
        for k in range(GROUP):
            start = order_ref[step * GROUP + k] * block_cols
            shift = lax.rem(2 * LANES - lax.rem(start, LANES), 2 * LANES)
            pair = jnp.concatenate([refs[2 * k][...], refs[2 * k + 1][...]], axis=1)
            out_ref[:, k * block_cols : (k + 1) * block_cols] = pltpu.roll(pair, shift, 1)[:, :block_cols]

    in_specs = []
    for k in range(GROUP):
        in_specs.append(pl.BlockSpec((rows, LANES), lambda g, o, k=k: (0, first_tile(o[g * GROUP + k]))))
        in_specs.append(
            pl.BlockSpec((rows, LANES), lambda g, o, k=k: (0, jnp.minimum(first_tile(o[g * GROUP + k]) + 1, last_tile)))
        )
    return pl.pallas_call(
        body,
        out_shape=jax.ShapeDtypeStruct((rows, count * block_cols), f32),
        grid_spec=pltpu.PrefetchScalarGridSpec(
            num_scalar_prefetch=1,
            grid=(count // GROUP,),
            in_specs=in_specs,
            out_specs=pl.BlockSpec((rows, GROUP * block_cols), lambda g, o: (0, g)),
        ),
        compiler_params=params(),
        cost_estimate=pl.CostEstimate(flops=0, bytes_accessed=5 * rows * count * LANES * 4, transcendentals=0),
        name="reorder_integrals",
    )(order, *([integrals] * (2 * GROUP)))


def split(x):
    high = x.astype(bf16)
    return high, (x - high.astype(f32)).astype(bf16)


def contract(parts, panels, eps_row, eps_occ):
    rows, cols = parts[0].shape
    tile = 5 * LANES
    width = panels.shape[1]
    half = width // 2

    def body(a_ref, b_ref, c_ref, d_ref, p_ref, v_ref, o_ref, own_ref, other_ref):
        x_high, x_low = split(jnp.concatenate([a_ref[...], b_ref[...], c_ref[...], d_ref[...]], axis=0))
        p_high, p_low = split(p_ref[...])
        dims = (((0,), (0,)), ((), ()))
        dot = functools.partial(lax.dot_general, dimension_numbers=dims, preferred_element_type=f32)
        ladder = dot(x_high, p_high) + (dot(x_high, p_low) + dot(x_low, p_high))
        eps = jnp.broadcast_to(v_ref[...], (8, tile)).T[:, :1]
        scaled = ladder / (eps - o_ref[...])
        own_ref[...] = scaled[:, :half]
        other_ref[...] = scaled[:, half:]

    part_spec = pl.BlockSpec((rows, tile), lambda g: (0, g))
    out_spec = pl.BlockSpec((tile, half), lambda g: (g, 0))
    out = jax.ShapeDtypeStruct((cols, half), f32)
    return pl.pallas_call(
        body,
        out_shape=(out, out),
        grid=(cols // tile,),
        in_specs=[part_spec] * 4
        + [
            pl.BlockSpec(panels.shape, lambda g: (0, 0)),
            pl.BlockSpec((1, tile), lambda g: (0, g)),
            pl.BlockSpec((1, width), lambda g: (0, 0)),
        ],
        out_specs=(out_spec, out_spec),
        compiler_params=params(),
        cost_estimate=pl.CostEstimate(
            flops=6 * 4 * rows * cols * width,
            bytes_accessed=4 * (4 * rows * cols + 4 * rows * width + cols * width),
            transcendentals=0,
        ),
        name="contract_scale",
    )(*parts, panels, eps_row, eps_occ)


def pack(computed, received, is_end, group_of_owner, senders):
    size = computed.shape[1:]

    def body(table_ref, a_ref, b_ref, out_ref):
        out_ref[...] = jnp.where(table_ref[senders] > 0, b_ref[...], a_ref[...])

    table = jnp.concatenate([group_of_owner, is_end[None]]).astype(jnp.int32)
    spec_a = pl.BlockSpec((1,) + size, lambda g, t: (t[g] * (1 - t[senders]), 0, 0))
    spec_b = pl.BlockSpec((1,) + size, lambda g, t: (t[g] * t[senders], 0, 0))
    return pl.pallas_call(
        body,
        out_shape=jax.ShapeDtypeStruct((senders,) + size, f32),
        grid_spec=pltpu.PrefetchScalarGridSpec(
            num_scalar_prefetch=1,
            grid=(senders,),
            in_specs=[spec_a, spec_b],
            out_specs=pl.BlockSpec((1,) + size, lambda g, t: (g, 0, 0)),
        ),
        compiler_params=params(),
        cost_estimate=pl.CostEstimate(flops=0, bytes_accessed=8 * senders * size[0] * size[1], transcendentals=0),
        name="pack_blocks",
    )(table, computed, received)


def place(arrived, result, source, target):
    count = source.shape[0]
    size = arrived.shape[1:]

    def body(s_ref, t_ref, a_ref, *rest):
        rest[-1][...] = a_ref[...]

    in_specs = [pl.BlockSpec((1,) + size, lambda g, s, t: (s[g], 0, 0))]
    args = [source, target, arrived]
    aliases = {}
    if result is not None:
        in_specs.append(pl.BlockSpec(memory_space=pl.ANY))
        args.append(result)
        aliases = {3: 0}
    return pl.pallas_call(
        body,
        out_shape=jax.ShapeDtypeStruct((NB_DEV,) + size, f32),
        grid_spec=pltpu.PrefetchScalarGridSpec(
            num_scalar_prefetch=2,
            grid=(count,),
            in_specs=in_specs,
            out_specs=pl.BlockSpec((1,) + size, lambda g, s, t: (t[g], 0, 0)),
        ),
        input_output_aliases=aliases,
        compiler_params=params(),
        cost_estimate=pl.CostEstimate(flops=0, bytes_accessed=8 * count * size[0] * size[1], transcendentals=0),
        name="place_blocks",
    )(*args)


def gather_panels(amplitudes, panel_owner, device_id, senders, occ_id, occ_size):
    rows, width = amplitudes.shape
    piece = rows // senders
    owner_of_row = jnp.repeat(panel_owner, rows // STEPS)
    masked = jnp.where((owner_of_row == device_id)[:, None], amplitudes, 0.0).reshape(senders, piece, width)
    shares = lax.all_to_all(masked, "vir", split_axis=0, concat_axis=0, tiled=True)
    share = jnp.sum(shares, axis=0)
    outer = lax.ppermute(share, "occ", [(0, 1), (occ_size - 1, occ_size - 2)])
    gathered = jnp.concatenate([share, outer], axis=1)[None]
    bit = senders // 2
    chunk_ids = device_id[None]
    while bit:
        received = lax.ppermute(gathered, "vir", [(i, i ^ bit) for i in range(senders)])
        gathered = jnp.concatenate([gathered, received], axis=0)
        chunk_ids = jnp.concatenate([chunk_ids, chunk_ids ^ bit])
        bit //= 2
    slab = senders // occ_size
    slabs = jnp.stack([occ_id, occ_id - 1, occ_id + 1, jnp.where(occ_id < 2, 3, 0)]) % occ_size
    wanted = (slabs[:, None] * slab + jnp.arange(slab)[None, :]).reshape(-1)
    where_is = jnp.sum(
        jnp.where(chunk_ids[None, :] == wanted[:, None], jnp.arange(senders)[None, :], 0), axis=1
    )
    return gathered[where_is].reshape(rows, 2 * width)


def local(amplitudes, integrals, eps_vir, eps_occ, panel_owner, block_target):
    device_id = lax.axis_index("vir")
    occ_id = lax.axis_index("occ")
    senders = lax.axis_size("vir")
    occ_size = lax.axis_size("occ")
    last = occ_size - 1
    is_end = (occ_id == 0) | (occ_id == last)
    capacity = max(2, 2 * NB_DEV // senders)
    chunks = min(CHUNKS, capacity)
    fanout = NB_DEV // capacity
    in_chunk = NB_DEV // chunks
    block_cols = eps_vir.shape[0] // NB_DEV
    width = eps_occ.shape[0]

    order, group_of_owner, source, target = routing(block_target, device_id, senders, capacity, chunks)
    eps_rows = eps_vir.reshape(NB_DEV, block_cols)[order].reshape(chunks, 1, in_chunk * block_cols)
    eps_other = lax.ppermute(eps_occ, "occ", [(0, 1), (last, last - 1)])
    eps_both = jnp.concatenate([eps_occ, eps_other])[None]
    panels = gather_panels(amplitudes, panel_owner, device_id, senders, occ_id, occ_size)

    inner_up = [(0, 1), (1, 2)]
    inner_down = [(3, 2), (2, 1)]
    outer = [(0, 2), (3, 1)]
    result = None
    for j in range(chunks):
        span = slice(j * in_chunk, (j + 1) * in_chunk)
        own = reorder(integrals, order[span], block_cols)
        below = lax.ppermute(own, "occ", inner_up)
        above = lax.ppermute(own, "occ", inner_down)
        far = lax.ppermute(own, "occ", outer)
        mine, others = contract([own, below, above, far], panels, eps_rows[j], eps_both)
        received = lax.ppermute(others, "occ", [(1, 0), (2, 3)])
        grouped = (fanout, in_chunk * block_cols // fanout, width)
        buffer = pack(mine.reshape(grouped), received.reshape(grouped), is_end, group_of_owner, senders)
        arrived = lax.all_to_all(buffer, "vir", split_axis=0, concat_axis=0, tiled=True)
        arrived = arrived.reshape(-1, block_cols, width)
        result = place(arrived, result, source[span], target[span])
    return result.reshape(NB_DEV * block_cols, width)


def solution(mesh):
    in_specs = (P("vir", "occ"), P("occ", "vir"), P("vir"), P("occ"), P(), P())
    out_specs = P("vir", "occ")
    return jax.shard_map(local, mesh=mesh, in_specs=in_specs, out_specs=out_specs, check_vma=False)
```

```python
import functools
import math

import jax
import jax.numpy as jnp
from jax import lax
from jax.experimental import pallas as pl
from jax.experimental.pallas import tpu as pltpu
from jax.sharding import PartitionSpec as P

STEPS = 12
NB_DEV = 64
LANES = 128
HALF = LANES // 2
VMEM_LIMIT = 58 * 1024 * 1024

f32 = jnp.float32
bf16 = jnp.bfloat16
ANY = pl.BlockSpec(memory_space=pl.ANY)


def params():
    return pltpu.CompilerParams(vmem_limit_bytes=VMEM_LIMIT)


def cheap():
    return pl.CostEstimate(flops=0, bytes_accessed=1024, transcendentals=0)


def routing(block_target, device_id, senders, capacity):
    fanout = NB_DEV // capacity
    place = jnp.arange(NB_DEV)
    ids = jnp.arange(senders)
    few = jnp.arange(fanout)
    owners = (block_target // NB_DEV).reshape(senders, NB_DEV)
    same = owners[:, :, None] == owners[:, None, :]
    rank = jnp.sum((same & (place[None, None, :] < place[None, :, None])).astype(jnp.int32), axis=2)

    mine = lax.dynamic_index_in_dim(owners, device_id, 0, keepdims=False)
    my_rank = lax.dynamic_index_in_dim(rank, device_id, 0, keepdims=False)
    ordinal = jnp.sum((mine[None, :] < mine[:, None]).astype(jnp.int32), axis=1) // capacity
    position = my_rank * fanout + ordinal
    order = jnp.sum(jnp.where(position[None, :] == place[:, None], place[None, :], 0), axis=1)
    first = (my_rank == 0)[None, :] & (ordinal[None, :] == few[:, None])
    owner_list = jnp.sum(jnp.where(first, mine[None, :], 0), axis=1)

    to_me = owners == device_id
    sends = (jnp.sum(to_me.astype(jnp.int32), axis=1) > 0).astype(jnp.int32)
    earlier = jnp.sum(jnp.where(ids[None, :] < ids[:, None], sends[None, :], 0), axis=1)
    listed = (sends[None, :] > 0) & (earlier[None, :] == few[:, None])
    sender_list = jnp.sum(jnp.where(listed, ids[None, :], 0), axis=1)
    entry = jnp.where(to_me, rank * fanout + earlier[:, None], -1).reshape(-1)
    hit = entry[None, :] == place[:, None]
    source = jnp.sum(jnp.where(hit, jnp.arange(senders * NB_DEV)[None, :], 0), axis=1)
    target = jnp.sum(jnp.where(hit, (block_target % NB_DEV)[None, :], 0), axis=1)
    return order, owner_list, sender_list, source, target


def block_copies(pairs, sems):
    copies = [pltpu.make_async_copy(src, dst, sems.at[k]) for k, (src, dst) in enumerate(pairs)]
    for copy in copies:
        copy.start()
    for copy in copies:
        copy.wait()


def pack(integrals, order, dest, slots, block_cols, after):
    rows, cols = integrals.shape
    count = order.shape[0]
    fold = block_cols // 2
    height = block_cols + fold
    last_tile = cols // LANES - 1

    def first_tile(block):
        return lax.div(block * block_cols, LANES)

    def body(order_ref, dest_ref, *refs):
        out_ref, units, sems = refs[-3:]
        copies = []
        for k in range(count):
            offset = lax.rem(order_ref[k] * block_cols, LANES)
            pair = jnp.concatenate([refs[2 * k][...], refs[2 * k + 1][...]], axis=1)
            aligned = pltpu.roll(pair, lax.rem(2 * LANES - offset, 2 * LANES), 1)[:, :LANES]
            folded = pltpu.roll(pair[LANES:], 2 * LANES - offset - fold, 1)[:, :LANES]
            units[k, :block_cols, :] = aligned[:LANES].T[:block_cols]
            units[k, block_cols:, :] = jnp.concatenate([aligned[LANES:], folded], axis=0).T[:fold]
            copy = pltpu.make_async_copy(units.at[k], out_ref.at[dest_ref[k]], sems.at[k])
            copy.start()
            copies.append(copy)
        for copy in copies:
            copy.wait()

    in_specs = []
    for k in range(count):
        in_specs.append(pl.BlockSpec((rows, LANES), lambda g, o, d, k=k: (0, first_tile(o[k]))))
        in_specs.append(
            pl.BlockSpec((rows, LANES), lambda g, o, d, k=k: (0, jnp.minimum(first_tile(o[k]) + 1, last_tile)))
        )
    return pl.pallas_call(
        body,
        out_shape=jax.ShapeDtypeStruct((slots, height, LANES), f32),
        grid_spec=pltpu.PrefetchScalarGridSpec(
            num_scalar_prefetch=2,
            grid=(1,),
            in_specs=in_specs + [ANY] * len(after),
            out_specs=ANY,
            scratch_shapes=[pltpu.VMEM((count, height, LANES), f32), pltpu.SemaphoreType.DMA((count,))],
        ),
        compiler_params=params(),
        cost_estimate=cheap(),
        name="pack_integrals",
    )(order, dest, *([integrals] * (2 * count)), *after)


def spread(blocks, dest, slots, alternative, use_alternative, result, after, name):
    count = dest.shape[0]
    size = blocks.shape[1:]
    table = jnp.concatenate([dest, use_alternative.astype(jnp.int32)[None]])
    extra = list(after) + ([result] if result is not None else [])

    def body(table_ref, a_ref, b_ref, *refs):
        out_ref, sems = refs[-2:]

        @pl.when(table_ref[count] == 0)
        def _():
            block_copies([(a_ref.at[k], out_ref.at[table_ref[k]]) for k in range(count)], sems)

        @pl.when(table_ref[count] != 0)
        def _():
            block_copies([(b_ref.at[k], out_ref.at[table_ref[k]]) for k in range(count)], sems)

    return pl.pallas_call(
        body,
        out_shape=jax.ShapeDtypeStruct((slots,) + size, f32),
        grid_spec=pltpu.PrefetchScalarGridSpec(
            num_scalar_prefetch=1,
            grid=(1,),
            in_specs=[ANY] * (2 + len(extra)),
            out_specs=ANY,
            scratch_shapes=[pltpu.SemaphoreType.DMA((count,))],
        ),
        input_output_aliases={2 + len(extra): 0} if result is not None else {},
        compiler_params=params(),
        cost_estimate=cheap(),
        name=name,
    )(table, blocks, alternative, *extra)


def collect(blocks, source, dest, result, after, name):
    count = source.shape[0]
    size = blocks.shape[1:]
    table = source if dest is None else jnp.concatenate([source, dest])
    slots = count if dest is None else NB_DEV
    extra = list(after) + ([result] if result is not None else [])

    def body(table_ref, a_ref, *refs):
        out_ref, sems = refs[-2:]
        places = [k if dest is None else table_ref[count + k] for k in range(count)]
        block_copies([(a_ref.at[table_ref[k]], out_ref.at[places[k]]) for k in range(count)], sems)

    return pl.pallas_call(
        body,
        out_shape=jax.ShapeDtypeStruct((slots,) + size, f32),
        grid_spec=pltpu.PrefetchScalarGridSpec(
            num_scalar_prefetch=1,
            grid=(1,),
            in_specs=[ANY] * (1 + len(extra)),
            out_specs=ANY,
            scratch_shapes=[pltpu.SemaphoreType.DMA((count,))],
        ),
        input_output_aliases={1 + len(extra): 0} if result is not None else {},
        compiler_params=params(),
        cost_estimate=cheap(),
        name=name,
    )(table, blocks, *extra)


def split(x):
    high = x.astype(bf16)
    return high, (x - high.astype(f32)).astype(bf16)


def contract(parts, panels, eps_row, eps_occ, block_cols, after):
    count, height, _ = parts[0].shape
    rows = count * block_cols
    fold = height - block_cols
    width = panels.shape[1]
    half = width // 2

    def body(a_ref, b_ref, c_ref, d_ref, p_ref, v_ref, o_ref, *refs):
        own_ref, other_ref = refs[-2:]
        sources = [ref[...] for ref in (a_ref, b_ref, c_ref, d_ref)]
        pieces = [x[:, :block_cols].reshape(rows, LANES) for x in sources]
        tails = [x[:, block_cols:] for x in sources]
        low_lanes = lax.broadcasted_iota(jnp.int32, (count, fold, LANES), 2) < HALF
        for x, y in ((tails[0], tails[1]), (tails[2], tails[3])):
            upper = jnp.where(low_lanes, x, pltpu.roll(y, HALF, 2))
            lower = jnp.where(low_lanes, pltpu.roll(x, HALF, 2), y)
            pieces.append(jnp.concatenate([upper, lower], axis=1).reshape(rows, LANES))
        x_high, x_low = split(jnp.concatenate(pieces, axis=1))
        p_high, p_low = split(p_ref[...])
        dot = functools.partial(jnp.dot, preferred_element_type=f32)
        ladder = dot(x_high, p_high) + (dot(x_high, p_low) + dot(x_low, p_high))
        eps = jnp.broadcast_to(v_ref[...], (8, rows)).T[:, :1]
        scaled = ladder / (eps - o_ref[...])
        own_ref[...] = scaled[:, :half].reshape(count, block_cols, half)
        other_ref[...] = scaled[:, half:].reshape(count, block_cols, half)

    out_spec = pl.BlockSpec((count, block_cols, half), lambda g: (0, 0, 0))
    out = jax.ShapeDtypeStruct((count, block_cols, half), f32)
    return pl.pallas_call(
        body,
        out_shape=(out, out),
        grid=(1,),
        in_specs=[pl.BlockSpec(parts[0].shape, lambda g: (0, 0, 0))] * 4
        + [
            pl.BlockSpec(panels.shape, lambda g: (0, 0)),
            pl.BlockSpec((1, rows), lambda g: (0, 0)),
            pl.BlockSpec((1, width), lambda g: (0, 0)),
        ]
        + [ANY] * len(after),
        out_specs=(out_spec, out_spec),
        compiler_params=params(),
        cost_estimate=cheap(),
        name="contract_scale",
    )(*parts, panels, eps_row, eps_occ, *after)


def own_rows(amplitudes, panel_owner, device_id, after):
    rows, width = amplitudes.shape
    panel = rows // STEPS

    def body(table_ref, a_ref, *refs):
        out_ref = refs[-1]
        for s in range(STEPS):
            rows_of = slice(s * panel, (s + 1) * panel)
            keep = table_ref[s] == table_ref[STEPS]
            out_ref[rows_of, :] = jnp.where(keep, a_ref[rows_of, :], 0.0)

    table = jnp.concatenate([panel_owner, device_id[None]]).astype(jnp.int32)
    whole = pl.BlockSpec((rows, width), lambda g, t: (0, 0))
    return pl.pallas_call(
        body,
        out_shape=jax.ShapeDtypeStruct((rows, width), f32),
        grid_spec=pltpu.PrefetchScalarGridSpec(
            num_scalar_prefetch=1, grid=(1,), in_specs=[whole] + [ANY] * len(after), out_specs=whole
        ),
        compiler_params=params(),
        cost_estimate=cheap(),
        name="own_panel_rows",
    )(table, amplitudes, *after)


def gather_panels(masked, device_id, senders, occ_id, occ_size):
    rows, width = masked.shape
    piece = rows // senders
    shares = lax.all_to_all(masked.reshape(senders, piece, width), "vir", split_axis=0, concat_axis=0, tiled=True)
    share = jnp.sum(shares, axis=0)
    outer = lax.ppermute(share, "occ", [(0, 1), (occ_size - 1, occ_size - 2)])
    gathered = jnp.concatenate([share, outer], axis=1)[None]
    bit = senders // 2
    piece_ids = device_id[None]
    while bit:
        received = lax.ppermute(gathered, "vir", [(i, i ^ bit) for i in range(senders)])
        gathered = jnp.concatenate([gathered, received], axis=0)
        piece_ids = jnp.concatenate([piece_ids, piece_ids ^ bit])
        bit //= 2
    grain = math.gcd(HALF, piece)
    grains = rows // grain
    slab = rows // occ_size
    slabs = jnp.stack([occ_id, occ_id - 1, occ_id + 1, jnp.where(occ_id < 2, 3, 0)]) % occ_size
    main = slabs[:, None] * (slab // grain) + jnp.arange(LANES // grain)[None, :]
    tail = slabs[:, None] * (slab // grain) + LANES // grain + jnp.arange(HALF // grain)[None, :]
    wanted = jnp.concatenate([main.reshape(-1), tail.reshape(-1)])
    per_piece = piece // grain
    holds = piece_ids[:, None] * per_piece + jnp.arange(per_piece)[None, :]
    hit = holds.reshape(-1)[None, :] == wanted[:, None]
    where_is = jnp.sum(jnp.where(hit, jnp.arange(grains)[None, :], 0), axis=1)
    return gathered.reshape(grains, grain, 2 * width)[where_is].reshape(rows, 2 * width)


def local(amplitudes, integrals, eps_vir, eps_occ, panel_owner, block_target):
    device_id = lax.axis_index("vir")
    occ_id = lax.axis_index("occ")
    senders = lax.axis_size("vir")
    occ_size = lax.axis_size("occ")
    last = occ_size - 1
    is_end = (occ_id == 0) | (occ_id == last)
    never = jnp.zeros((), jnp.bool_)
    capacity = max(2, 2 * NB_DEV // senders)
    fanout = NB_DEV // capacity
    block_cols = eps_vir.shape[0] // NB_DEV
    width = eps_occ.shape[0]
    if capacity >= 8:
        plan = [2] * (capacity // 2 - 1) + [1, 1]
    else:
        plan = [1] * capacity
    late = 2 if len(plan) > 4 else 1
    firsts = [sum(plan[:j]) for j in range(len(plan))]

    order, owner_list, sender_list, source, target = routing(block_target, device_id, senders, capacity)

    def span(j):
        return slice(firsts[j] * fanout, (firsts[j] + plan[j]) * fanout)

    def slot_places(listed, j):
        return (listed[None, :] * plan[j] + jnp.arange(plan[j])[:, None]).reshape(-1)

    def exchange(z):
        below = lax.ppermute(z, "occ", [(0, 1), (1, 2)])
        above = lax.ppermute(z, "occ", [(3, 2), (2, 1)])
        far = lax.ppermute(z, "occ", [(0, 2), (3, 1)])
        return [z, below, above, far]

    def route(buffer, j):
        size = buffer.shape[1:]
        buffer = buffer.reshape((senders, plan[j] * size[0]) + size[1:])
        arrived = lax.all_to_all(buffer, "vir", split_axis=0, concat_axis=0, tiled=True)
        return arrived.reshape((senders * plan[j],) + size)

    n = len(plan)
    chunks, packed = {}, {}
    for j in range(late):
        count = plan[j] * fanout
        z = pack(integrals, order[span(j)], jnp.arange(count), count, block_cols, [])
        chunks[j] = exchange(z)
    packed[late] = pack(
        integrals, order[span(late)], slot_places(owner_list, late), senders * plan[late], block_cols, [chunks[late - 1][0]]
    )

    masked = own_rows(amplitudes, panel_owner, device_id, [chunks[0][0]])
    panels = gather_panels(masked, device_id, senders, occ_id, occ_size)
    eps_other = lax.ppermute(eps_occ, "occ", [(0, 1), (last, last - 1)])
    eps_both = jnp.concatenate([eps_occ, eps_other])[None]
    eps_all = lax.all_gather(eps_vir, "vir", axis=0, tiled=True).reshape(-1, block_cols)
    near = firsts[late] * fanout
    eps_rows = eps_all[jnp.concatenate([device_id * NB_DEV + order[:near], source[near:]])]

    def send(j):
        if j + 1 < n:
            places = slot_places(owner_list, j + 1)
            packed[j + 1] = pack(integrals, order[span(j + 1)], places, senders * plan[j + 1], block_cols, [packed[j]])
        after = [packed[j + 1]] if j + 1 < n else []
        after += chunks[j - 2][1:] if j >= 2 else []
        z = collect(route(packed[j], j), slot_places(sender_list, j), None, None, after, "compact_integrals")
        chunks[j] = exchange(z)

    result = None
    returning = {}
    for j in range(n):
        if j == 0:
            for k in range(late, min(late + 1, n)):
                send(k)
        elif j + 2 < n and j + 2 not in chunks:
            send(j + 2)
        after = [chunks[j + 2][0]] if j + 2 < n else []
        if result is not None:
            after.append(result)
        eps_row = eps_rows[span(j)].reshape(1, -1)
        mine, others = contract(chunks[j], panels, eps_row, eps_both, block_cols, after)
        received = lax.ppermute(others, "occ", [(1, 0), (2, 3)])
        if j < late:
            places = slot_places(owner_list, j)
            buffer = spread(mine, places, senders * plan[j], received, is_end, None, [], "pack_results")
            returning[j] = route(buffer, j)
        else:
            result = spread(mine, target[span(j)], NB_DEV, received, is_end, result, [], "place_results")
        if j - late in returning:
            k = j - late
            places = slot_places(sender_list, k)
            result = collect(returning[k], places, target[span(k)], result, [], "place_returned")
            del returning[k]
    return result.reshape(NB_DEV * block_cols, width)


def solution(mesh):
    in_specs = (P("vir", "occ"), P("occ", "vir"), P("vir"), P("occ"), P(), P())
    out_specs = P("vir", "occ")
    return jax.shard_map(local, mesh=mesh, in_specs=in_specs, out_specs=out_specs, check_vma=False)
```

```python
import functools
import math

import jax
import jax.numpy as jnp
from jax import lax
from jax.experimental import pallas as pl
from jax.experimental.pallas import tpu as pltpu
from jax.sharding import PartitionSpec as P

STEPS = 12
NB_DEV = 64
LANES = 128
HALF = LANES // 2
VMEM_LIMIT = 58 * 1024 * 1024

f32 = jnp.float32
bf16 = jnp.bfloat16
ANY = pl.BlockSpec(memory_space=pl.ANY)


def params():
    return pltpu.CompilerParams(vmem_limit_bytes=VMEM_LIMIT)


def cheap():
    return pl.CostEstimate(flops=0, bytes_accessed=1024, transcendentals=0)


def routing(block_target, device_id, senders, capacity):
    fanout = NB_DEV // capacity
    place = jnp.arange(NB_DEV)
    ids = jnp.arange(senders)
    few = jnp.arange(fanout)
    owners = (block_target // NB_DEV).reshape(senders, NB_DEV)
    same = owners[:, :, None] == owners[:, None, :]
    rank = jnp.sum((same & (place[None, None, :] < place[None, :, None])).astype(jnp.int32), axis=2)

    mine = lax.dynamic_index_in_dim(owners, device_id, 0, keepdims=False)
    my_rank = lax.dynamic_index_in_dim(rank, device_id, 0, keepdims=False)
    ordinal = jnp.sum((mine[None, :] < mine[:, None]).astype(jnp.int32), axis=1) // capacity
    position = my_rank * fanout + ordinal
    order = jnp.sum(jnp.where(position[None, :] == place[:, None], place[None, :], 0), axis=1)
    first = (my_rank == 0)[None, :] & (ordinal[None, :] == few[:, None])
    owner_list = jnp.sum(jnp.where(first, mine[None, :], 0), axis=1)

    to_me = owners == device_id
    sends = (jnp.sum(to_me.astype(jnp.int32), axis=1) > 0).astype(jnp.int32)
    earlier = jnp.sum(jnp.where(ids[None, :] < ids[:, None], sends[None, :], 0), axis=1)
    listed = (sends[None, :] > 0) & (earlier[None, :] == few[:, None])
    sender_list = jnp.sum(jnp.where(listed, ids[None, :], 0), axis=1)
    entry = jnp.where(to_me, rank * fanout + earlier[:, None], -1).reshape(-1)
    hit = entry[None, :] == place[:, None]
    source = jnp.sum(jnp.where(hit, jnp.arange(senders * NB_DEV)[None, :], 0), axis=1)
    target = jnp.sum(jnp.where(hit, (block_target % NB_DEV)[None, :], 0), axis=1)
    return order, owner_list, sender_list, source, target


def block_copies(pairs, held, sems):
    loads = [pltpu.make_async_copy(src, held.at[k], sems.at[0, k]) for k, (src, _) in enumerate(pairs)]
    stores = [pltpu.make_async_copy(held.at[k], dst, sems.at[1, k]) for k, (_, dst) in enumerate(pairs)]
    for load in loads:
        load.start()
    for load, store in zip(loads, stores):
        load.wait()
        store.start()
    for store in stores:
        store.wait()


def copy_scratch(count, size):
    return [pltpu.VMEM((count,) + size, f32), pltpu.SemaphoreType.DMA((2, count))]


def pack(integrals, order, dest, slots, block_cols, after):
    rows, cols = integrals.shape
    count = order.shape[0]
    fold = block_cols // 2
    height = block_cols + fold
    last_tile = cols // LANES - 1

    def first_tile(block):
        return lax.div(block * block_cols, LANES)

    def body(order_ref, dest_ref, *refs):
        out_ref, units, sems = refs[-3:]
        copies = []
        for k in range(count):
            offset = lax.rem(order_ref[k] * block_cols, LANES)
            pair = jnp.concatenate([refs[2 * k][...], refs[2 * k + 1][...]], axis=1)
            aligned = pltpu.roll(pair, lax.rem(2 * LANES - offset, 2 * LANES), 1)[:, :LANES]
            folded = pltpu.roll(pair[LANES:], 2 * LANES - offset - fold, 1)[:, :LANES]
            units[k, :block_cols, :] = aligned[:LANES].T[:block_cols]
            units[k, block_cols:, :] = jnp.concatenate([aligned[LANES:], folded], axis=0).T[:fold]
            copy = pltpu.make_async_copy(units.at[k], out_ref.at[dest_ref[k]], sems.at[k])
            copy.start()
            copies.append(copy)
        for copy in copies:
            copy.wait()

    in_specs = []
    for k in range(count):
        in_specs.append(pl.BlockSpec((rows, LANES), lambda g, o, d, k=k: (0, first_tile(o[k]))))
        in_specs.append(
            pl.BlockSpec((rows, LANES), lambda g, o, d, k=k: (0, jnp.minimum(first_tile(o[k]) + 1, last_tile)))
        )
    return pl.pallas_call(
        body,
        out_shape=jax.ShapeDtypeStruct((slots, height, LANES), f32),
        grid_spec=pltpu.PrefetchScalarGridSpec(
            num_scalar_prefetch=2,
            grid=(1,),
            in_specs=in_specs + [ANY] * len(after),
            out_specs=ANY,
            scratch_shapes=[pltpu.VMEM((count, height, LANES), f32), pltpu.SemaphoreType.DMA((count,))],
        ),
        compiler_params=params(),
        cost_estimate=cheap(),
        name="pack_integrals",
    )(order, dest, *([integrals] * (2 * count)), *after)


def spread(blocks, dest, slots, alternative, use_alternative, result, after, name):
    count = dest.shape[0]
    size = blocks.shape[1:]
    table = jnp.concatenate([dest, use_alternative.astype(jnp.int32)[None]])
    extra = list(after) + ([result] if result is not None else [])

    def body(table_ref, a_ref, b_ref, *refs):
        out_ref, held, sems = refs[-3:]

        @pl.when(table_ref[count] == 0)
        def _():
            block_copies([(a_ref.at[k], out_ref.at[table_ref[k]]) for k in range(count)], held, sems)

        @pl.when(table_ref[count] != 0)
        def _():
            block_copies([(b_ref.at[k], out_ref.at[table_ref[k]]) for k in range(count)], held, sems)

    return pl.pallas_call(
        body,
        out_shape=jax.ShapeDtypeStruct((slots,) + size, f32),
        grid_spec=pltpu.PrefetchScalarGridSpec(
            num_scalar_prefetch=1,
            grid=(1,),
            in_specs=[ANY] * (2 + len(extra)),
            out_specs=ANY,
            scratch_shapes=copy_scratch(count, size),
        ),
        input_output_aliases={2 + len(extra): 0} if result is not None else {},
        compiler_params=params(),
        cost_estimate=cheap(),
        name=name,
    )(table, blocks, alternative, *extra)


def collect(blocks, source, dest, result, after, name):
    count = source.shape[0]
    size = blocks.shape[1:]
    table = source if dest is None else jnp.concatenate([source, dest])
    slots = count if dest is None else NB_DEV
    extra = list(after) + ([result] if result is not None else [])

    def body(table_ref, a_ref, *refs):
        out_ref, held, sems = refs[-3:]
        places = [k if dest is None else table_ref[count + k] for k in range(count)]
        block_copies([(a_ref.at[table_ref[k]], out_ref.at[places[k]]) for k in range(count)], held, sems)

    return pl.pallas_call(
        body,
        out_shape=jax.ShapeDtypeStruct((slots,) + size, f32),
        grid_spec=pltpu.PrefetchScalarGridSpec(
            num_scalar_prefetch=1,
            grid=(1,),
            in_specs=[ANY] * (1 + len(extra)),
            out_specs=ANY,
            scratch_shapes=copy_scratch(count, size),
        ),
        input_output_aliases={1 + len(extra): 0} if result is not None else {},
        compiler_params=params(),
        cost_estimate=cheap(),
        name=name,
    )(table, blocks, *extra)


def split(x):
    high = x.astype(bf16)
    return high, (x - high.astype(f32)).astype(bf16)


def contract(parts, panels, eps_row, eps_occ, block_cols, after):
    count, height, _ = parts[0].shape
    rows = count * block_cols
    fold = height - block_cols
    width = panels.shape[1]
    half = width // 2

    def body(a_ref, b_ref, c_ref, d_ref, p_ref, v_ref, o_ref, *refs):
        own_ref, other_ref = refs[-2:]
        sources = [ref[...] for ref in (a_ref, b_ref, c_ref, d_ref)]
        pieces = [x[:, :block_cols].reshape(rows, LANES) for x in sources]
        tails = [x[:, block_cols:] for x in sources]
        low_lanes = lax.broadcasted_iota(jnp.int32, (count, fold, LANES), 2) < HALF
        for x, y in ((tails[0], tails[1]), (tails[2], tails[3])):
            upper = jnp.where(low_lanes, x, pltpu.roll(y, HALF, 2))
            lower = jnp.where(low_lanes, pltpu.roll(x, HALF, 2), y)
            pieces.append(jnp.concatenate([upper, lower], axis=1).reshape(rows, LANES))
        x_high, x_low = split(jnp.concatenate(pieces, axis=1))
        p_high, p_low = split(p_ref[...])
        dot = functools.partial(jnp.dot, preferred_element_type=f32)
        ladder = dot(x_high, p_high) + (dot(x_high, p_low) + dot(x_low, p_high))
        eps = jnp.broadcast_to(v_ref[...], (8, rows)).T[:, :1]
        scaled = ladder / (eps - o_ref[...])
        own_ref[...] = scaled[:, :half].reshape(count, block_cols, half)
        other_ref[...] = scaled[:, half:].reshape(count, block_cols, half)

    out_spec = pl.BlockSpec((count, block_cols, half), lambda g: (0, 0, 0))
    out = jax.ShapeDtypeStruct((count, block_cols, half), f32)
    return pl.pallas_call(
        body,
        out_shape=(out, out),
        grid=(1,),
        in_specs=[pl.BlockSpec(parts[0].shape, lambda g: (0, 0, 0))] * 4
        + [
            pl.BlockSpec(panels.shape, lambda g: (0, 0)),
            pl.BlockSpec((1, rows), lambda g: (0, 0)),
            pl.BlockSpec((1, width), lambda g: (0, 0)),
        ]
        + [ANY] * len(after),
        out_specs=(out_spec, out_spec),
        compiler_params=params(),
        cost_estimate=cheap(),
        name="contract_scale",
    )(*parts, panels, eps_row, eps_occ, *after)


def own_rows(amplitudes, panel_owner, device_id, after):
    rows, width = amplitudes.shape
    panel = rows // STEPS

    def body(table_ref, a_ref, *refs):
        out_ref = refs[-1]
        for s in range(STEPS):
            rows_of = slice(s * panel, (s + 1) * panel)
            keep = table_ref[s] == table_ref[STEPS]
            out_ref[rows_of, :] = jnp.where(keep, a_ref[rows_of, :], 0.0)

    table = jnp.concatenate([panel_owner, device_id[None]]).astype(jnp.int32)
    whole = pl.BlockSpec((rows, width), lambda g, t: (0, 0))
    return pl.pallas_call(
        body,
        out_shape=jax.ShapeDtypeStruct((rows, width), f32),
        grid_spec=pltpu.PrefetchScalarGridSpec(
            num_scalar_prefetch=1, grid=(1,), in_specs=[whole] + [ANY] * len(after), out_specs=whole
        ),
        compiler_params=params(),
        cost_estimate=cheap(),
        name="own_panel_rows",
    )(table, amplitudes, *after)


def gather_panels(masked, device_id, senders, occ_id, occ_size):
    rows, width = masked.shape
    piece = rows // senders
    shares = lax.all_to_all(masked.reshape(senders, piece, width), "vir", split_axis=0, concat_axis=0, tiled=True)
    share = jnp.sum(shares, axis=0)
    outer = lax.ppermute(share, "occ", [(0, 1), (occ_size - 1, occ_size - 2)])
    gathered = jnp.concatenate([share, outer], axis=1)[None]
    bit = senders // 2
    piece_ids = device_id[None]
    while bit:
        received = lax.ppermute(gathered, "vir", [(i, i ^ bit) for i in range(senders)])
        gathered = jnp.concatenate([gathered, received], axis=0)
        piece_ids = jnp.concatenate([piece_ids, piece_ids ^ bit])
        bit //= 2
    grain = math.gcd(HALF, piece)
    grains = rows // grain
    slab = rows // occ_size
    slabs = jnp.stack([occ_id, occ_id - 1, occ_id + 1, jnp.where(occ_id < 2, 3, 0)]) % occ_size
    main = slabs[:, None] * (slab // grain) + jnp.arange(LANES // grain)[None, :]
    tail = slabs[:, None] * (slab // grain) + LANES // grain + jnp.arange(HALF // grain)[None, :]
    wanted = jnp.concatenate([main.reshape(-1), tail.reshape(-1)])
    per_piece = piece // grain
    holds = piece_ids[:, None] * per_piece + jnp.arange(per_piece)[None, :]
    hit = holds.reshape(-1)[None, :] == wanted[:, None]
    where_is = jnp.sum(jnp.where(hit, jnp.arange(grains)[None, :], 0), axis=1)
    return gathered.reshape(grains, grain, 2 * width)[where_is].reshape(rows, 2 * width)


def local(amplitudes, integrals, eps_vir, eps_occ, panel_owner, block_target):
    device_id = lax.axis_index("vir")
    occ_id = lax.axis_index("occ")
    senders = lax.axis_size("vir")
    occ_size = lax.axis_size("occ")
    last = occ_size - 1
    is_end = (occ_id == 0) | (occ_id == last)
    never = jnp.zeros((), jnp.bool_)
    capacity = max(2, 2 * NB_DEV // senders)
    fanout = NB_DEV // capacity
    block_cols = eps_vir.shape[0] // NB_DEV
    width = eps_occ.shape[0]
    if capacity >= 8:
        plan = [2] * (capacity // 2 - 1) + [1, 1]
    else:
        plan = [1] * capacity
    late = 2 if len(plan) > 4 else 1
    firsts = [sum(plan[:j]) for j in range(len(plan))]

    order, owner_list, sender_list, source, target = routing(block_target, device_id, senders, capacity)

    def span(j):
        return slice(firsts[j] * fanout, (firsts[j] + plan[j]) * fanout)

    def slot_places(listed, j):
        return (listed[None, :] * plan[j] + jnp.arange(plan[j])[:, None]).reshape(-1)

    def exchange(z):
        below = lax.ppermute(z, "occ", [(0, 1), (1, 2)])
        above = lax.ppermute(z, "occ", [(3, 2), (2, 1)])
        far = lax.ppermute(z, "occ", [(0, 2), (3, 1)])
        return [z, below, above, far]

    def route(buffer, j):
        size = buffer.shape[1:]
        buffer = buffer.reshape((senders, plan[j] * size[0]) + size[1:])
        arrived = lax.all_to_all(buffer, "vir", split_axis=0, concat_axis=0, tiled=True)
        return arrived.reshape((senders * plan[j],) + size)

    n = len(plan)
    chunks, packed = {}, {}
    for j in range(late):
        count = plan[j] * fanout
        z = pack(integrals, order[span(j)], jnp.arange(count), count, block_cols, [])
        chunks[j] = exchange(z)
    packed[late] = pack(
        integrals, order[span(late)], slot_places(owner_list, late), senders * plan[late], block_cols, [chunks[late - 1][0]]
    )

    masked = own_rows(amplitudes, panel_owner, device_id, [chunks[0][0]])
    panels = gather_panels(masked, device_id, senders, occ_id, occ_size)
    eps_other = lax.ppermute(eps_occ, "occ", [(0, 1), (last, last - 1)])
    eps_both = jnp.concatenate([eps_occ, eps_other])[None]
    eps_all = lax.all_gather(eps_vir, "vir", axis=0, tiled=True).reshape(-1, block_cols)
    near = firsts[late] * fanout
    eps_rows = eps_all[jnp.concatenate([device_id * NB_DEV + order[:near], source[near:]])]

    def send(j):
        if j + 1 < n:
            places = slot_places(owner_list, j + 1)
            packed[j + 1] = pack(integrals, order[span(j + 1)], places, senders * plan[j + 1], block_cols, [packed[j]])
        after = [packed[j + 1]] if j + 1 < n else []
        after += chunks[j - 2][1:] if j >= 2 else []
        z = collect(route(packed[j], j), slot_places(sender_list, j), None, None, after, "compact_integrals")
        chunks[j] = exchange(z)

    result = None
    returning = {}
    for j in range(n):
        if j == 0:
            for k in range(late, min(late + 1, n)):
                send(k)
        elif j + 2 < n and j + 2 not in chunks:
            send(j + 2)
        after = [chunks[j + 2][0]] if j + 2 < n else []
        if result is not None:
            after.append(result)
        eps_row = eps_rows[span(j)].reshape(1, -1)
        mine, others = contract(chunks[j], panels, eps_row, eps_both, block_cols, after)
        received = lax.ppermute(others, "occ", [(1, 0), (2, 3)])
        if j < late:
            places = slot_places(owner_list, j)
            buffer = spread(mine, places, senders * plan[j], received, is_end, None, [], "pack_results")
            returning[j] = route(buffer, j)
        else:
            result = spread(mine, target[span(j)], NB_DEV, received, is_end, result, [], "place_results")
        if j - late in returning:
            k = j - late
            places = slot_places(sender_list, k)
            result = collect(returning[k], places, target[span(k)], result, [], "place_returned")
            del returning[k]
    return result.reshape(NB_DEV * block_cols, width)


def solution(mesh):
    in_specs = (P("vir", "occ"), P("occ", "vir"), P("vir"), P("occ"), P(), P())
    out_specs = P("vir", "occ")
    return jax.shard_map(local, mesh=mesh, in_specs=in_specs, out_specs=out_specs, check_vma=False)
```

```python
import functools
import math

import jax
import jax.numpy as jnp
from jax import lax
from jax.experimental import pallas as pl
from jax.experimental.pallas import tpu as pltpu
from jax.sharding import PartitionSpec as P

STEPS = 12
NB_DEV = 64
LANES = 128
HALF = LANES // 2
GROUPS = 8
VMEM_LIMIT = 62 * 1024 * 1024

f32 = jnp.float32
bf16 = jnp.bfloat16
ANY = pl.BlockSpec(memory_space=pl.ANY)


def params():
    return pltpu.CompilerParams(vmem_limit_bytes=VMEM_LIMIT)


def cheap():
    return pl.CostEstimate(flops=0, bytes_accessed=1024, transcendentals=0)


def routing(block_target, device_id, senders, capacity, is_end):
    fanout = NB_DEV // capacity
    place = jnp.arange(NB_DEV)
    ids = jnp.arange(senders)
    few = jnp.arange(fanout)
    owners = (block_target // NB_DEV).reshape(senders, NB_DEV)
    same = owners[:, :, None] == owners[:, None, :]
    rank = jnp.sum((same & (place[None, None, :] < place[None, :, None])).astype(jnp.int32), axis=2)

    mine = lax.dynamic_index_in_dim(owners, device_id, 0, keepdims=False)
    my_rank = lax.dynamic_index_in_dim(rank, device_id, 0, keepdims=False)
    ordinal = jnp.sum((mine[None, :] < mine[:, None]).astype(jnp.int32), axis=1) // capacity
    position = my_rank * fanout + ordinal
    order = jnp.sum(jnp.where(position[None, :] == place[:, None], place[None, :], 0), axis=1)
    first = (my_rank == 0)[None, :] & (ordinal[None, :] == few[:, None])
    owner_list = jnp.sum(jnp.where(first, mine[None, :], 0), axis=1)

    to_me = owners == device_id
    sends = (jnp.sum(to_me.astype(jnp.int32), axis=1) > 0).astype(jnp.int32)
    earlier = jnp.sum(jnp.where(ids[None, :] < ids[:, None], sends[None, :], 0), axis=1)
    listed = (sends[None, :] > 0) & (earlier[None, :] == few[:, None])
    sender_list = jnp.sum(jnp.where(listed, ids[None, :], 0), axis=1)
    entry = jnp.where(to_me, rank * fanout + earlier[:, None], -1).reshape(-1)
    hit = entry[None, :] == place[:, None]
    source = jnp.sum(jnp.where(hit, jnp.arange(senders * NB_DEV)[None, :], 0), axis=1)
    target = jnp.sum(jnp.where(hit, (block_target % NB_DEV)[None, :], 0), axis=1)
    table = jnp.concatenate([order, target, owner_list, sender_list, is_end.astype(jnp.int32)[None]])
    return table, order, source


class Layout:
    def __init__(self, senders, block_cols):
        self.senders = senders
        self.block_cols = block_cols
        self.height = block_cols + block_cols // 2
        self.capacity = max(2, 2 * NB_DEV // senders)
        self.fanout = NB_DEV // self.capacity
        self.plan = [4, 4, 2, 2, 2, 1, 1] if self.capacity == 16 else [1] * self.capacity
        self.groups = [[1], [2, 3], [4, 5, 6]] if self.capacity == 16 else [[j] for j in range(1, self.capacity)]
        self.firsts = [sum(self.plan[:j]) for j in range(len(self.plan))]

    def blocks(self, j):
        for rank in range(self.firsts[j], self.firsts[j] + self.plan[j]):
            for few in range(self.fanout):
                yield rank * self.fanout + few, rank, few

    def count(self, j):
        return self.plan[j] * self.fanout

    def order(self, table, position):
        return table[position]

    def target(self, table, position):
        return table[NB_DEV + position]

    def owner(self, table, few):
        return table[2 * NB_DEV + few]

    def sender(self, table, few):
        return table[2 * NB_DEV + self.fanout + few]

    def is_end(self, table):
        return table[2 * NB_DEV + 2 * self.fanout]

    def bundle(self, chunks):
        return self.firsts[chunks[0]], sum(self.plan[j] for j in chunks)


def kernel_call(body, out_shape, scalars, in_specs, out_specs, args, name, scratch=(), grid=(1,), aliases=None):
    return pl.pallas_call(
        body,
        out_shape=out_shape,
        grid_spec=pltpu.PrefetchScalarGridSpec(
            num_scalar_prefetch=len(scalars),
            grid=grid,
            in_specs=in_specs,
            out_specs=out_specs,
            scratch_shapes=list(scratch),
        ),
        input_output_aliases=aliases or {},
        compiler_params=params(),
        cost_estimate=cheap(),
        name=name,
    )(*scalars, *args)


def start_all(copies):
    for copy in copies:
        copy.start()


def wait_all(copies):
    for copy in copies:
        copy.wait()


def prepare(table, owners, integrals, amplitudes, layout):
    rows, cols = integrals.shape
    block_cols, height = layout.block_cols, layout.height
    fold = height - block_cols
    stretch = cols // GROUPS
    tiles = stretch // LANES
    per_stretch = stretch // block_cols
    panel = amplitudes.shape[0] // STEPS
    moves = [(0, position, few, position) for position, _, few in layout.blocks(0)]
    shapes = [layout.count(0)]
    for g, chunks in enumerate(layout.groups):
        first, ranks = layout.bundle(chunks)
        shapes.append(layout.senders * ranks)
        for j in chunks:
            moves += [(g + 1, position, few, (ranks, rank - first)) for position, rank, few in layout.blocks(j)]

    def body(table_ref, owner_ref, x_ref, a_ref, *refs):
        masked_ref = refs[0]
        outs = refs[1 : 1 + len(shapes)]
        x, units, load_sems, store_sems = refs[1 + len(shapes) :]
        loads = []
        for s in range(GROUPS):
            part = pl.ds(s * stretch, stretch)
            loads.append(pltpu.make_async_copy(x_ref.at[:, part], x.at[:, part], load_sems.at[s]))
        start_all(loads)
        for s in range(STEPS):
            part = slice(s * panel, (s + 1) * panel)
            masked_ref[part, :] = jnp.where(owner_ref[s] == owner_ref[STEPS], a_ref[part, :], 0.0)
        for s in range(GROUPS):
            loads[s].wait()
            for t in range(tiles):
                lanes = slice(s * stretch + t * LANES, s * stretch + (t + 1) * LANES)
                main = x[:LANES, lanes].T
                rest = x[LANES:, lanes]
                tail = jnp.concatenate([rest, rest], axis=0).T
                at = t * LANES
                while at < (t + 1) * LANES:
                    block, row = divmod(at, block_cols)
                    stop = min((t + 1) * LANES, (block + 1) * block_cols, block * block_cols + (fold if row < fold else block_cols))
                    size = stop - at
                    here = slice(at - t * LANES, stop - t * LANES)
                    unit = s * per_stretch + block
                    units[unit, row : row + size, :] = main[here]
                    if row < fold:
                        units[unit, block_cols + row : block_cols + row + size, :HALF] = tail[here, :HALF]
                    else:
                        low = block_cols + row - fold
                        units[unit, low : low + size, HALF:] = tail[here, HALF:]
                    at = stop
        stores = []
        for k, (which, position, few, place) in enumerate(moves):
            if which:
                place = layout.owner(table_ref, few) * place[0] + place[1]
            source = units.at[layout.order(table_ref, position)]
            stores.append(pltpu.make_async_copy(source, outs[which].at[place], store_sems.at[k]))
        start_all(stores)
        wait_all(stores)

    whole = pl.BlockSpec(amplitudes.shape, lambda g, t, o: (0, 0))
    out = [jax.ShapeDtypeStruct((count, height, LANES), f32) for count in shapes]
    return kernel_call(
        body,
        [jax.ShapeDtypeStruct(amplitudes.shape, f32)] + out,
        [table, owners],
        [ANY, whole],
        [whole] + [ANY] * len(out),
        [integrals, amplitudes],
        "prepare_integrals",
        [
            pltpu.VMEM((rows, cols), f32),
            pltpu.VMEM((NB_DEV, height, LANES), f32),
            pltpu.SemaphoreType.DMA((GROUPS,)),
            pltpu.SemaphoreType.DMA((len(moves),)),
        ],
    )


def compact(table, arrived, layout, j, chunks, after):
    first, ranks = layout.bundle(chunks)
    count = layout.count(j)
    size = arrived.shape[1:]

    def body(table_ref, a_ref, *refs):
        out_ref, held, sems = refs[-3:]
        loads, stores = [], []
        for k, (_, rank, few) in enumerate(layout.blocks(j)):
            source = a_ref.at[layout.sender(table_ref, few) * ranks + rank - first]
            loads.append(pltpu.make_async_copy(source, held.at[k], sems.at[0, k]))
            stores.append(pltpu.make_async_copy(held.at[k], out_ref.at[k], sems.at[1, k]))
        start_all(loads)
        for load, store in zip(loads, stores):
            load.wait()
            store.start()
        wait_all(stores)

    return kernel_call(
        body,
        jax.ShapeDtypeStruct((count,) + size, f32),
        [table],
        [ANY] * (1 + len(after)),
        ANY,
        [arrived, *after],
        "compact_integrals",
        [pltpu.VMEM((count,) + size, f32), pltpu.SemaphoreType.DMA((2, count))],
    )


def pack_results(table, mine, received, layout, j):
    count = layout.count(j)
    ranks = layout.plan[j]
    size = mine.shape[1:]

    def body(table_ref, a_ref, b_ref, out_ref, held, sems):
        loads_a, loads_b, stores = [], [], []
        for k, (_, rank, few) in enumerate(layout.blocks(j)):
            place = layout.owner(table_ref, few) * ranks + rank - layout.firsts[j]
            loads_a.append(pltpu.make_async_copy(a_ref.at[k], held.at[k], sems.at[0, k]))
            loads_b.append(pltpu.make_async_copy(b_ref.at[k], held.at[k], sems.at[0, k]))
            stores.append(pltpu.make_async_copy(held.at[k], out_ref.at[place], sems.at[1, k]))
        pl.when(layout.is_end(table_ref) == 0)(lambda: start_all(loads_a))
        pl.when(layout.is_end(table_ref) != 0)(lambda: start_all(loads_b))
        for load, store in zip(loads_a, stores):
            load.wait()
            store.start()
        wait_all(stores)

    return kernel_call(
        body,
        jax.ShapeDtypeStruct((layout.senders * ranks,) + size, f32),
        [table],
        [ANY] * 2,
        ANY,
        [mine, received],
        "pack_results",
        [pltpu.VMEM((count,) + size, f32), pltpu.SemaphoreType.DMA((2, count))],
    )


class Placing:
    def __init__(self, layout, jobs):
        self.layout = layout
        self.jobs = jobs
        self.arrays = [array for _, arrays in jobs for array in arrays]
        self.count = sum(layout.count(j) for j, _ in jobs)
        self.size = (layout.block_cols, self.arrays[0].shape[-1]) if jobs else None

    def scratch(self):
        return [pltpu.VMEM((self.count,) + self.size, f32), pltpu.SemaphoreType.DMA((2, self.count))] if self.jobs else []

    def copies(self, table, refs, out, held, sems):
        layout = self.layout
        options = ([], [])
        stores = []
        refs = list(refs)
        k = 0
        for j, arrays in self.jobs:
            mine = refs[: len(arrays)]
            refs = refs[len(arrays) :]
            for index, (position, rank, few) in enumerate(layout.blocks(j)):
                if len(arrays) == 2:
                    sources = (mine[0].at[index], mine[1].at[index])
                else:
                    place = layout.sender(table, few) * layout.plan[j] + rank - layout.firsts[j]
                    sources = (mine[0].at[place],) * 2
                for option, source in zip(options, sources):
                    option.append(pltpu.make_async_copy(source, held.at[k], sems.at[0, k]))
                stores.append(pltpu.make_async_copy(held.at[k], out.at[layout.target(table, position)], sems.at[1, k]))
                k += 1
        return options, stores

    def load(self, table, options):
        pl.when(self.layout.is_end(table) == 0)(lambda: start_all(options[0]))
        pl.when(self.layout.is_end(table) != 0)(lambda: start_all(options[1]))

    def store(self, options, stores):
        for load, store in zip(options[0], stores):
            load.wait()
            store.start()


def place(table, result, layout, jobs):
    placing = Placing(layout, jobs)

    def body(table_ref, *refs):
        out_ref, held, sems = refs[-3:]
        options, stores = placing.copies(table_ref, refs[: len(placing.arrays)], out_ref, held, sems)
        placing.load(table_ref, options)
        placing.store(options, stores)
        wait_all(stores)

    return kernel_call(
        body,
        jax.ShapeDtypeStruct((NB_DEV,) + placing.size, f32),
        [table],
        [ANY] * (len(placing.arrays) + (result is not None)),
        ANY,
        placing.arrays + ([result] if result is not None else []),
        "place_results",
        placing.scratch(),
        aliases={1 + len(placing.arrays): 0} if result is not None else None,
    )


def split(x):
    high = x.astype(bf16)
    return high, (x - high.astype(f32)).astype(bf16)


def contract(table, parts, panels, eps, eps_occ, layout, j, result, jobs, after):
    count, height, _ = parts[0].shape
    block_cols = layout.block_cols
    step = layout.fanout if layout.fanout < 8 else 8
    rows = step * block_cols
    fold = height - block_cols
    width = panels.shape[1]
    half = width // 2
    steps = count // step
    start = layout.firsts[j] * layout.fanout // step
    placing = Placing(layout, jobs)
    n_jobs = len(placing.arrays)

    def body(table_ref, a_ref, b_ref, c_ref, d_ref, p_ref, v_ref, o_ref, *refs):
        refs, p_high, p_low = refs[:-2], refs[-2], refs[-1]
        g = pl.program_id(0)
        if jobs:
            refs, (held, sems) = refs[:-2], refs[-2:]
            own_ref, other_ref, out_ref = refs[-3:]
            options, stores = placing.copies(table_ref, refs[:n_jobs], out_ref, held, sems)
            pl.when(g == 0)(lambda: placing.load(table_ref, options))
        else:
            own_ref, other_ref = refs[-2:]

        @pl.when(g == 0)
        def _():
            p_high[...], p_low[...] = split(p_ref[...])

        sources = [ref[...] for ref in (a_ref, b_ref, c_ref, d_ref)]
        pieces = [x[:, :block_cols].reshape(rows, LANES) for x in sources]
        tails = [x[:, block_cols:] for x in sources]
        low_lanes = lax.broadcasted_iota(jnp.int32, (step, fold, LANES), 2) < HALF
        for x, y in ((tails[0], tails[1]), (tails[2], tails[3])):
            upper = jnp.where(low_lanes, x, pltpu.roll(y, HALF, 2))
            lower = jnp.where(low_lanes, pltpu.roll(x, HALF, 2), y)
            pieces.append(jnp.concatenate([upper, lower], axis=1).reshape(rows, LANES))
        x_high, x_low = split(jnp.concatenate(pieces, axis=1))
        dot = functools.partial(jnp.dot, preferred_element_type=f32)
        ladder = dot(x_high, p_high[...]) + (dot(x_high, p_low[...]) + dot(x_low, p_high[...]))
        eps_cols = jnp.concatenate([v_ref[0]] * (8 // step), axis=0).T
        for b in range(step):
            scaled = ladder[b * block_cols : (b + 1) * block_cols] / (eps_cols[:, b : b + 1] - o_ref[...])
            own_ref[b] = scaled[:, :half]
            other_ref[b] = scaled[:, half:]
        if jobs:

            @pl.when(g == steps - 1)
            def _():
                placing.store(options, stores)
                wait_all(stores)

    out_spec = pl.BlockSpec((step, block_cols, half), lambda g, t: (g, 0, 0))
    out = jax.ShapeDtypeStruct((count, block_cols, half), f32)
    out_shape, out_specs = [out, out], [out_spec, out_spec]
    extra = list(after)
    aliases = None
    if jobs:
        out_shape.append(jax.ShapeDtypeStruct((NB_DEV,) + placing.size, f32))
        out_specs.append(ANY)
        if result is not None:
            extra.append(result)
            aliases = {7 + n_jobs + len(extra): 0 + 2}
    outs = kernel_call(
        body,
        out_shape,
        [table],
        [pl.BlockSpec((step, height, LANES), lambda g, t: (g, 0, 0))] * 4
        + [
            pl.BlockSpec(panels.shape, lambda g, t: (0, 0)),
            pl.BlockSpec((1, step, block_cols), lambda g, t: (start + g, 0, 0)),
            pl.BlockSpec((1, width), lambda g, t: (0, 0)),
        ]
        + [ANY] * (n_jobs + len(extra)),
        out_specs,
        [*parts, panels, eps.reshape(NB_DEV // step, step, block_cols), eps_occ, *placing.arrays, *extra],
        "contract_scale",
        placing.scratch() + [pltpu.VMEM(panels.shape, bf16), pltpu.VMEM(panels.shape, bf16)],
        grid=(steps,),
        aliases=aliases,
    )
    return (*outs, result) if not jobs else tuple(outs)


def gather_small(masked, eps_vir, eps_occ, device_id, senders, occ_id, occ_size):
    rows, width = masked.shape
    piece = rows // senders
    shares = lax.all_to_all(masked.reshape(senders, piece, width), "vir", split_axis=0, concat_axis=0, tiled=True)
    share = jnp.concatenate([jnp.sum(shares, axis=0), jnp.broadcast_to(eps_occ[None], (8, width))], axis=0)
    outer = lax.ppermute(share, "occ", [(0, 1), (occ_size - 1, occ_size - 2)])
    both = jnp.concatenate([share, outer], axis=1)
    eps_both = both[piece : piece + 1]
    eps_rows = eps_vir.shape[0] // (2 * width)
    spare = -(piece + eps_rows) % 8
    own_eps = jnp.pad(eps_vir.reshape(eps_rows, 2 * width), ((0, spare), (0, 0)))
    gathered = jnp.concatenate([both[:piece], own_eps], axis=0)[None]
    bit = senders // 2
    piece_ids = device_id[None]
    while bit:
        received = lax.ppermute(gathered, "vir", [(i, i ^ bit) for i in range(senders)])
        gathered = jnp.concatenate([gathered, received], axis=0)
        piece_ids = jnp.concatenate([piece_ids, piece_ids ^ bit])
        bit //= 2
    grain = math.gcd(HALF, piece)
    grains = rows // grain
    slab = rows // occ_size
    slabs = jnp.stack([occ_id, occ_id - 1, occ_id + 1, jnp.where(occ_id < 2, 3, 0)]) % occ_size
    main = slabs[:, None] * (slab // grain) + jnp.arange(LANES // grain)[None, :]
    tail = slabs[:, None] * (slab // grain) + LANES // grain + jnp.arange(HALF // grain)[None, :]
    wanted = jnp.concatenate([main.reshape(-1), tail.reshape(-1)])
    per_piece = piece // grain
    holds = piece_ids[:, None] * per_piece + jnp.arange(per_piece)[None, :]
    hit = holds.reshape(-1)[None, :] == wanted[:, None]
    where_is = jnp.sum(jnp.where(hit, jnp.arange(grains)[None, :], 0), axis=1)
    panels = gathered[:, :piece].reshape(grains, grain, 2 * width)[where_is].reshape(rows, 2 * width)
    eps_all = gathered[:, piece : piece + eps_rows].reshape(senders, eps_vir.shape[0])
    return panels, eps_all, piece_ids, eps_both


def local(amplitudes, integrals, eps_vir, eps_occ, panel_owner, block_target):
    device_id = lax.axis_index("vir")
    occ_id = lax.axis_index("occ")
    senders = lax.axis_size("vir")
    occ_size = lax.axis_size("occ")
    is_end = (occ_id == 0) | (occ_id == occ_size - 1)
    layout = Layout(senders, eps_vir.shape[0] // NB_DEV)
    block_cols, width = layout.block_cols, eps_occ.shape[0]
    table, order, source = routing(block_target, device_id, senders, layout.capacity, is_end)

    def exchange(z):
        below = lax.ppermute(z, "occ", [(0, 1), (1, 2)])
        above = lax.ppermute(z, "occ", [(3, 2), (2, 1)])
        far = lax.ppermute(z, "occ", [(0, 2), (3, 1)])
        return [z, below, above, far]

    def route(buffer):
        size = buffer.shape[1:]
        ranks = buffer.shape[0] // senders
        buffer = buffer.reshape((senders, ranks * size[0]) + size[1:])
        arrived = lax.all_to_all(buffer, "vir", split_axis=0, concat_axis=0, tiled=True)
        return arrived.reshape((senders * ranks,) + size)

    owners = jnp.concatenate([panel_owner, device_id[None]]).astype(jnp.int32)
    masked, first, *buffers = prepare(table, owners, integrals, amplitudes, layout)
    chunks = {0: exchange(first)}
    panels, eps_all, piece_ids, eps_both = gather_small(
        masked, eps_vir, eps_occ, device_id, senders, occ_id, occ_size
    )
    near = layout.count(0)
    listed = jnp.concatenate([device_id * NB_DEV + order[:near], source[near:]])
    hit = (listed // NB_DEV)[:, None] == piece_ids[None, :]
    listed = jnp.sum(jnp.where(hit, jnp.arange(senders)[None, :], 0), axis=1) * NB_DEV + listed % NB_DEV
    eps = eps_all.reshape(senders * NB_DEV, block_cols)[listed]

    n = len(layout.plan)
    group_of = {j: g for g, group in enumerate(layout.groups) for j in group}
    arrived = [route(buffer) for buffer in buffers]
    for j in range(1, n):
        g = group_of[j]
        after = chunks[j - 2][1:] if j >= 2 else []
        chunks[j] = exchange(compact(table, arrived[g], layout, j, layout.groups[g], after))

    result = None
    pending = []
    returned = None
    for j in range(n):
        after = [chunks[j + 2][0]] if 1 <= j and j + 2 < n else []
        jobs = [job for job in pending if job[0] <= j - 2]
        if j == 4:
            jobs += [returned]
        pending = [job for job in pending if job[0] > j - 2]
        mine, others, result = contract(
            table, chunks[j], panels, eps, eps_both, layout, j, result, jobs, after
        )
        received = lax.ppermute(others, "occ", [(1, 0), (2, 3)])
        if j == 0:
            returned = (0, [route(pack_results(table, mine, received, layout, 0))])
            if n < 5:
                pending.append(returned)
        else:
            pending.append((j, [mine, received]))
    result = place(table, result, layout, pending)
    return result.reshape(NB_DEV * block_cols, width)


def solution(mesh):
    in_specs = (P("vir", "occ"), P("occ", "vir"), P("vir"), P("occ"), P(), P())
    out_specs = P("vir", "occ")
    return jax.shard_map(local, mesh=mesh, in_specs=in_specs, out_specs=out_specs, check_vma=False)
```

```python
import functools
import math

import jax
import jax.numpy as jnp
from jax import lax
from jax.experimental import pallas as pl
from jax.experimental.pallas import tpu as pltpu
from jax.sharding import PartitionSpec as P

STEPS = 12
NB_DEV = 64
LANES = 128
HALF = LANES // 2
GROUPS = 8
VMEM_LIMIT = 62 * 1024 * 1024

f32 = jnp.float32
bf16 = jnp.bfloat16
ANY = pl.BlockSpec(memory_space=pl.ANY)


def params():
    return pltpu.CompilerParams(vmem_limit_bytes=VMEM_LIMIT)


def cheap():
    return pl.CostEstimate(flops=0, bytes_accessed=1024, transcendentals=0)


def routing(block_target, device_id, senders, capacity, is_end):
    fanout = NB_DEV // capacity
    place = jnp.arange(NB_DEV)
    ids = jnp.arange(senders)
    few = jnp.arange(fanout)
    owners = (block_target // NB_DEV).reshape(senders, NB_DEV)
    same = owners[:, :, None] == owners[:, None, :]
    rank = jnp.sum((same & (place[None, None, :] < place[None, :, None])).astype(jnp.int32), axis=2)

    mine = lax.dynamic_index_in_dim(owners, device_id, 0, keepdims=False)
    my_rank = lax.dynamic_index_in_dim(rank, device_id, 0, keepdims=False)
    ordinal = jnp.sum((mine[None, :] < mine[:, None]).astype(jnp.int32), axis=1) // capacity
    position = my_rank * fanout + ordinal
    order = jnp.sum(jnp.where(position[None, :] == place[:, None], place[None, :], 0), axis=1)
    first = (my_rank == 0)[None, :] & (ordinal[None, :] == few[:, None])
    owner_list = jnp.sum(jnp.where(first, mine[None, :], 0), axis=1)

    to_me = owners == device_id
    sends = (jnp.sum(to_me.astype(jnp.int32), axis=1) > 0).astype(jnp.int32)
    earlier = jnp.sum(jnp.where(ids[None, :] < ids[:, None], sends[None, :], 0), axis=1)
    listed = (sends[None, :] > 0) & (earlier[None, :] == few[:, None])
    sender_list = jnp.sum(jnp.where(listed, ids[None, :], 0), axis=1)
    entry = jnp.where(to_me, rank * fanout + earlier[:, None], -1).reshape(-1)
    hit = entry[None, :] == place[:, None]
    source = jnp.sum(jnp.where(hit, jnp.arange(senders * NB_DEV)[None, :], 0), axis=1)
    target = jnp.sum(jnp.where(hit, (block_target % NB_DEV)[None, :], 0), axis=1)
    table = jnp.concatenate([order, target, owner_list, sender_list, is_end.astype(jnp.int32)[None]])
    return table, order, source


class Layout:
    def __init__(self, senders, block_cols):
        self.senders = senders
        self.block_cols = block_cols
        self.height = block_cols + block_cols // 2
        self.capacity = max(2, 2 * NB_DEV // senders)
        self.fanout = NB_DEV // self.capacity
        self.plan = [4, 4, 2, 2, 2, 1, 1] if self.capacity == 16 else [1] * self.capacity
        self.groups = [[1, 2], [3], [4, 5, 6]] if self.capacity == 16 else [[j] for j in range(1, self.capacity)]
        self.firsts = [sum(self.plan[:j]) for j in range(len(self.plan))]

    def blocks(self, j):
        for rank in range(self.firsts[j], self.firsts[j] + self.plan[j]):
            for few in range(self.fanout):
                yield rank * self.fanout + few, rank, few

    def count(self, j):
        return self.plan[j] * self.fanout

    def order(self, table, position):
        return table[position]

    def target(self, table, position):
        return table[NB_DEV + position]

    def owner(self, table, few):
        return table[2 * NB_DEV + few]

    def sender(self, table, few):
        return table[2 * NB_DEV + self.fanout + few]

    def is_end(self, table):
        return table[2 * NB_DEV + 2 * self.fanout]

    def bundle(self, chunks):
        return self.firsts[chunks[0]], sum(self.plan[j] for j in chunks)


def kernel_call(body, out_shape, scalars, in_specs, out_specs, args, name, scratch=(), grid=(1,), aliases=None):
    return pl.pallas_call(
        body,
        out_shape=out_shape,
        grid_spec=pltpu.PrefetchScalarGridSpec(
            num_scalar_prefetch=len(scalars),
            grid=grid,
            in_specs=in_specs,
            out_specs=out_specs,
            scratch_shapes=list(scratch),
        ),
        input_output_aliases=aliases or {},
        compiler_params=params(),
        cost_estimate=cheap(),
        name=name,
    )(*scalars, *args)


def start_all(copies):
    for copy in copies:
        copy.start()


def wait_all(copies):
    for copy in copies:
        copy.wait()


def prepare(table, integrals, layout):
    rows, cols = integrals.shape
    block_cols, height = layout.block_cols, layout.height
    fold = height - block_cols
    stretch = cols // GROUPS
    tiles = stretch // LANES
    per_stretch = stretch // block_cols
    moves = [(0, position, few, position) for position, _, few in layout.blocks(0)]
    shapes = [layout.count(0)]
    for g, chunks in enumerate(layout.groups):
        first, ranks = layout.bundle(chunks)
        shapes.append(layout.senders * ranks)
        for j in chunks:
            moves += [(g + 1, position, few, (ranks, rank - first)) for position, rank, few in layout.blocks(j)]

    def body(table_ref, x_ref, *refs):
        outs = refs[: len(shapes)]
        x, units, load_sems, store_sems = refs[len(shapes) :]
        loads = []
        for s in range(GROUPS):
            part = pl.ds(s * stretch, stretch)
            loads.append(pltpu.make_async_copy(x_ref.at[:, part], x.at[:, part], load_sems.at[s]))
        start_all(loads)
        for s in range(GROUPS):
            loads[s].wait()
            for t in range(tiles):
                lanes = slice(s * stretch + t * LANES, s * stretch + (t + 1) * LANES)
                main = x[:LANES, lanes].T
                rest = x[LANES:, lanes]
                tail = jnp.concatenate([rest, rest], axis=0).T
                at = t * LANES
                while at < (t + 1) * LANES:
                    block, row = divmod(at, block_cols)
                    stop = min((t + 1) * LANES, (block + 1) * block_cols, block * block_cols + (fold if row < fold else block_cols))
                    size = stop - at
                    here = slice(at - t * LANES, stop - t * LANES)
                    unit = s * per_stretch + block
                    units[unit, row : row + size, :] = main[here]
                    if row < fold:
                        units[unit, block_cols + row : block_cols + row + size, :HALF] = tail[here, :HALF]
                    else:
                        low = block_cols + row - fold
                        units[unit, low : low + size, HALF:] = tail[here, HALF:]
                    at = stop
        stores = []
        for k, (which, position, few, place) in enumerate(moves):
            if which:
                place = layout.owner(table_ref, few) * place[0] + place[1]
            source = units.at[layout.order(table_ref, position)]
            stores.append(pltpu.make_async_copy(source, outs[which].at[place], store_sems.at[k]))
        start_all(stores)
        wait_all(stores)

    out = [jax.ShapeDtypeStruct((count, height, LANES), f32) for count in shapes]
    return kernel_call(
        body,
        out,
        [table],
        [ANY],
        [ANY] * len(out),
        [integrals],
        "prepare_integrals",
        [
            pltpu.VMEM((rows, cols), f32),
            pltpu.VMEM((NB_DEV, height, LANES), f32),
            pltpu.SemaphoreType.DMA((GROUPS,)),
            pltpu.SemaphoreType.DMA((len(moves),)),
        ],
    )


def compact(table, arrived, layout, j, chunks, after):
    first, ranks = layout.bundle(chunks)
    count = layout.count(j)
    size = arrived.shape[1:]

    def body(table_ref, a_ref, *refs):
        out_ref, held, sems = refs[-3:]
        loads, stores = [], []
        for k, (_, rank, few) in enumerate(layout.blocks(j)):
            source = a_ref.at[layout.sender(table_ref, few) * ranks + rank - first]
            loads.append(pltpu.make_async_copy(source, held.at[k], sems.at[0, k]))
            stores.append(pltpu.make_async_copy(held.at[k], out_ref.at[k], sems.at[1, k]))
        start_all(loads)
        for load, store in zip(loads, stores):
            load.wait()
            store.start()
        wait_all(stores)

    return kernel_call(
        body,
        jax.ShapeDtypeStruct((count,) + size, f32),
        [table],
        [ANY] * (1 + len(after)),
        ANY,
        [arrived, *after],
        "compact_integrals",
        [pltpu.VMEM((count,) + size, f32), pltpu.SemaphoreType.DMA((2, count))],
    )


def pack_results(table, mine, received, layout, j):
    count = layout.count(j)
    ranks = layout.plan[j]
    size = mine.shape[1:]

    def body(table_ref, a_ref, b_ref, out_ref, held, sems):
        loads_a, loads_b, stores = [], [], []
        for k, (_, rank, few) in enumerate(layout.blocks(j)):
            place = layout.owner(table_ref, few) * ranks + rank - layout.firsts[j]
            loads_a.append(pltpu.make_async_copy(a_ref.at[k], held.at[k], sems.at[0, k]))
            loads_b.append(pltpu.make_async_copy(b_ref.at[k], held.at[k], sems.at[0, k]))
            stores.append(pltpu.make_async_copy(held.at[k], out_ref.at[place], sems.at[1, k]))
        pl.when(layout.is_end(table_ref) == 0)(lambda: start_all(loads_a))
        pl.when(layout.is_end(table_ref) != 0)(lambda: start_all(loads_b))
        for load, store in zip(loads_a, stores):
            load.wait()
            store.start()
        wait_all(stores)

    return kernel_call(
        body,
        jax.ShapeDtypeStruct((layout.senders * ranks,) + size, f32),
        [table],
        [ANY] * 2,
        ANY,
        [mine, received],
        "pack_results",
        [pltpu.VMEM((count,) + size, f32), pltpu.SemaphoreType.DMA((2, count))],
    )


class Placing:
    def __init__(self, layout, jobs):
        self.layout = layout
        self.jobs = jobs
        self.arrays = [array for _, arrays in jobs for array in arrays]
        self.count = sum(layout.count(j) for j, _ in jobs)
        self.size = (layout.block_cols, self.arrays[0].shape[-1]) if jobs else None

    def scratch(self):
        return [pltpu.VMEM((self.count,) + self.size, f32), pltpu.SemaphoreType.DMA((2, self.count))] if self.jobs else []

    def copies(self, table, refs, out, held, sems):
        layout = self.layout
        options = ([], [])
        stores = []
        refs = list(refs)
        k = 0
        for j, arrays in self.jobs:
            mine = refs[: len(arrays)]
            refs = refs[len(arrays) :]
            for index, (position, rank, few) in enumerate(layout.blocks(j)):
                if len(arrays) == 2:
                    sources = (mine[0].at[index], mine[1].at[index])
                else:
                    place = layout.sender(table, few) * layout.plan[j] + rank - layout.firsts[j]
                    sources = (mine[0].at[place],) * 2
                for option, source in zip(options, sources):
                    option.append(pltpu.make_async_copy(source, held.at[k], sems.at[0, k]))
                stores.append(pltpu.make_async_copy(held.at[k], out.at[layout.target(table, position)], sems.at[1, k]))
                k += 1
        return options, stores

    def load(self, table, options):
        pl.when(self.layout.is_end(table) == 0)(lambda: start_all(options[0]))
        pl.when(self.layout.is_end(table) != 0)(lambda: start_all(options[1]))

    def store(self, options, stores):
        for load, store in zip(options[0], stores):
            load.wait()
            store.start()


def place(table, result, layout, jobs):
    placing = Placing(layout, jobs)

    def body(table_ref, *refs):
        out_ref, held, sems = refs[-3:]
        options, stores = placing.copies(table_ref, refs[: len(placing.arrays)], out_ref, held, sems)
        placing.load(table_ref, options)
        placing.store(options, stores)
        wait_all(stores)

    return kernel_call(
        body,
        jax.ShapeDtypeStruct((NB_DEV,) + placing.size, f32),
        [table],
        [ANY] * (len(placing.arrays) + (result is not None)),
        ANY,
        placing.arrays + ([result] if result is not None else []),
        "place_results",
        placing.scratch(),
        aliases={1 + len(placing.arrays): 0} if result is not None else None,
    )


def split(x):
    high = x.astype(bf16)
    return high, (x - high.astype(f32)).astype(bf16)


def contract(table, parts, panels, eps, eps_occ, layout, j, result, jobs, after):
    count, height, _ = parts[0].shape
    block_cols = layout.block_cols
    step = layout.fanout if layout.fanout < 8 else 8
    rows = step * block_cols
    fold = height - block_cols
    width = panels.shape[1]
    half = width // 2
    steps = count // step
    start = layout.firsts[j] * layout.fanout // step
    placing = Placing(layout, jobs)
    n_jobs = len(placing.arrays)

    def body(table_ref, a_ref, b_ref, c_ref, d_ref, p_ref, v_ref, o_ref, *refs):
        refs, p_high, p_low = refs[:-2], refs[-2], refs[-1]
        g = pl.program_id(0)
        if jobs:
            refs, (held, sems) = refs[:-2], refs[-2:]
            own_ref, other_ref, out_ref = refs[-3:]
            options, stores = placing.copies(table_ref, refs[:n_jobs], out_ref, held, sems)
            pl.when(g == 0)(lambda: placing.load(table_ref, options))
        else:
            own_ref, other_ref = refs[-2:]

        @pl.when(g == 0)
        def _():
            p_high[...], p_low[...] = split(p_ref[...])

        sources = [ref[...] for ref in (a_ref, b_ref, c_ref, d_ref)]
        pieces = [x[:, :block_cols].reshape(rows, LANES) for x in sources]
        tails = [x[:, block_cols:] for x in sources]
        low_lanes = lax.broadcasted_iota(jnp.int32, (step, fold, LANES), 2) < HALF
        for x, y in ((tails[0], tails[1]), (tails[2], tails[3])):
            upper = jnp.where(low_lanes, x, pltpu.roll(y, HALF, 2))
            lower = jnp.where(low_lanes, pltpu.roll(x, HALF, 2), y)
            pieces.append(jnp.concatenate([upper, lower], axis=1).reshape(rows, LANES))
        x_high, x_low = split(jnp.concatenate(pieces, axis=1))
        dot = functools.partial(jnp.dot, preferred_element_type=f32)
        ladder = dot(x_high, p_high[...]) + (dot(x_high, p_low[...]) + dot(x_low, p_high[...]))
        eps_cols = jnp.concatenate([v_ref[0]] * (8 // step), axis=0).T
        for b in range(step):
            scaled = ladder[b * block_cols : (b + 1) * block_cols] / (eps_cols[:, b : b + 1] - o_ref[...])
            own_ref[b] = scaled[:, :half]
            other_ref[b] = scaled[:, half:]
        if jobs:

            @pl.when(g == steps - 1)
            def _():
                placing.store(options, stores)
                wait_all(stores)

    out_spec = pl.BlockSpec((step, block_cols, half), lambda g, t: (g, 0, 0))
    out = jax.ShapeDtypeStruct((count, block_cols, half), f32)
    out_shape, out_specs = [out, out], [out_spec, out_spec]
    extra = list(after)
    aliases = None
    if jobs:
        out_shape.append(jax.ShapeDtypeStruct((NB_DEV,) + placing.size, f32))
        out_specs.append(ANY)
        if result is not None:
            extra.append(result)
            aliases = {7 + n_jobs + len(extra): 0 + 2}
    outs = kernel_call(
        body,
        out_shape,
        [table],
        [pl.BlockSpec((step, height, LANES), lambda g, t: (g, 0, 0))] * 4
        + [
            pl.BlockSpec(panels.shape, lambda g, t: (0, 0)),
            pl.BlockSpec((1, step, block_cols), lambda g, t: (start + g, 0, 0)),
            pl.BlockSpec((1, width), lambda g, t: (0, 0)),
        ]
        + [ANY] * (n_jobs + len(extra)),
        out_specs,
        [*parts, panels, eps.reshape(NB_DEV // step, step, block_cols), eps_occ, *placing.arrays, *extra],
        "contract_scale",
        placing.scratch() + [pltpu.VMEM(panels.shape, bf16), pltpu.VMEM(panels.shape, bf16)],
        grid=(steps,),
        aliases=aliases,
    )
    return (*outs, result) if not jobs else tuple(outs)


def own_rows(owners, amplitudes, after):
    panel = amplitudes.shape[0] // STEPS

    def body(owner_ref, a_ref, *refs):
        for s in range(STEPS):
            part = slice(s * panel, (s + 1) * panel)
            refs[-1][part, :] = jnp.where(owner_ref[s] == owner_ref[STEPS], a_ref[part, :], 0.0)

    whole = pl.BlockSpec(amplitudes.shape, lambda g, o: (0, 0))
    shape = jax.ShapeDtypeStruct(amplitudes.shape, f32)
    return kernel_call(
        body, shape, [owners], [whole] + [ANY] * len(after), whole, [amplitudes, *after], "own_panel_rows"
    )


def add_shares(shares, eps_occ, after):
    _, piece, width = shares.shape

    def body(s_ref, e_ref, *refs):
        refs[-1][:piece, :] = jnp.sum(s_ref[...], axis=0)
        refs[-1][piece:, :] = jnp.broadcast_to(e_ref[...], (8, width))

    shape = (piece + 8, width)
    return kernel_call(
        body,
        jax.ShapeDtypeStruct(shape, f32),
        [],
        [pl.BlockSpec(shares.shape, lambda g: (0, 0, 0)), pl.BlockSpec((1, width), lambda g: (0, 0))]
        + [ANY] * len(after),
        pl.BlockSpec(shape, lambda g: (0, 0)),
        [shares, eps_occ[None], *after],
        "add_shares",
    )


def join(first, second, after):
    size = first.shape[0]
    shape = (2 * size,) + first.shape[1:]

    def body(a_ref, b_ref, *refs):
        refs[-1][:size] = a_ref[...]
        refs[-1][size:] = b_ref[...]

    part = pl.BlockSpec(first.shape, lambda g: (0, 0, 0))
    return kernel_call(
        body,
        jax.ShapeDtypeStruct(shape, f32),
        [],
        [part, part] + [ANY] * len(after),
        pl.BlockSpec(shape, lambda g: (0, 0, 0)),
        [first, second, *after],
        "join_panels",
    )


def gather_small(masked, eps_vir, eps_occ, device_id, senders, occ_id, occ_size, waits):
    rows, width = masked.shape
    piece = rows // senders
    shares = lax.all_to_all(masked.reshape(senders, piece, width), "vir", split_axis=0, concat_axis=0, tiled=True)
    share = add_shares(shares, eps_occ, waits[0])
    outer = lax.ppermute(share, "occ", [(0, 1), (occ_size - 1, occ_size - 2)])
    both = jnp.concatenate([share, outer], axis=1)
    eps_both = both[piece : piece + 1]
    eps_rows = eps_vir.shape[0] // (2 * width)
    spare = -(piece + eps_rows) % 8
    own_eps = jnp.pad(eps_vir.reshape(eps_rows, 2 * width), ((0, spare), (0, 0)))
    gathered = jnp.concatenate([both[:piece], own_eps], axis=0)[None]
    bit = senders // 2
    piece_ids = device_id[None]
    while bit:
        received = lax.ppermute(gathered, "vir", [(i, i ^ bit) for i in range(senders)])
        waits = waits[1:]
        gathered = join(gathered, received, waits[0] if waits else [])
        piece_ids = jnp.concatenate([piece_ids, piece_ids ^ bit])
        bit //= 2
    grain = math.gcd(HALF, piece)
    grains = rows // grain
    slab = rows // occ_size
    near, far = jnp.where(occ_id < 2, 0, occ_size - 1), jnp.where(occ_id < 2, occ_size - 1, 0)
    slabs = jnp.stack([occ_id, near, occ_size - 1 - occ_id, far])
    main = slabs[:, None] * (slab // grain) + jnp.arange(LANES // grain)[None, :]
    tail = slabs[:, None] * (slab // grain) + LANES // grain + jnp.arange(HALF // grain)[None, :]
    wanted = jnp.concatenate([main.reshape(-1), tail.reshape(-1)])
    per_piece = piece // grain
    holds = piece_ids[:, None] * per_piece + jnp.arange(per_piece)[None, :]
    hit = holds.reshape(-1)[None, :] == wanted[:, None]
    where_is = jnp.sum(jnp.where(hit, jnp.arange(grains)[None, :], 0), axis=1)
    panels = gathered[:, :piece].reshape(grains, grain, 2 * width)[where_is].reshape(rows, 2 * width)
    eps_all = gathered[:, piece : piece + eps_rows].reshape(senders, eps_vir.shape[0])
    return panels, eps_all, piece_ids, eps_both


def local(amplitudes, integrals, eps_vir, eps_occ, panel_owner, block_target):
    device_id = lax.axis_index("vir")
    occ_id = lax.axis_index("occ")
    senders = lax.axis_size("vir")
    occ_size = lax.axis_size("occ")
    is_end = (occ_id == 0) | (occ_id == occ_size - 1)
    layout = Layout(senders, eps_vir.shape[0] // NB_DEV)
    block_cols, width = layout.block_cols, eps_occ.shape[0]
    table, order, source = routing(block_target, device_id, senders, layout.capacity, is_end)

    def exchange(z):
        outer = lax.ppermute(z, "occ", [(0, 1), (3, 2)])
        return [z, outer, lax.ppermute(z, "occ", [(1, 2), (2, 1)]), lax.ppermute(outer, "occ", [(1, 2), (2, 1)])]

    def route(buffer):
        size = buffer.shape[1:]
        ranks = buffer.shape[0] // senders
        buffer = buffer.reshape((senders, ranks * size[0]) + size[1:])
        arrived = lax.all_to_all(buffer, "vir", split_axis=0, concat_axis=0, tiled=True)
        return arrived.reshape((senders * ranks,) + size)

    first, *buffers = prepare(table, integrals, layout)
    n = len(layout.plan)
    group_of = {j: g for g, group in enumerate(layout.groups) for j in group}
    arrived = [route(buffer) for buffer in buffers]
    chunks = {0: exchange(first)}
    for j in range(1, n):
        g = group_of[j]
        chunks[j] = exchange(compact(table, arrived[g], layout, j, layout.groups[g], [chunks[j - 1][2]]))

    owners = jnp.concatenate([panel_owner, device_id[None]]).astype(jnp.int32)
    masked = own_rows(owners, amplitudes, [arrived[0]])
    waits = [chunks[0][1:], [chunks[1][0]], [chunks[1][1]]]
    panels, eps_all, piece_ids, eps_both = gather_small(
        masked, eps_vir, eps_occ, device_id, senders, occ_id, occ_size, waits
    )
    near = layout.count(0)
    listed = jnp.concatenate([device_id * NB_DEV + order[:near], source[near:]])
    hit = (listed // NB_DEV)[:, None] == piece_ids[None, :]
    listed = jnp.sum(jnp.where(hit, jnp.arange(senders)[None, :], 0), axis=1) * NB_DEV + listed % NB_DEV
    eps = eps_all.reshape(senders * NB_DEV, block_cols)[listed]

    result = None
    pending = []
    returned = None
    for j in range(n):
        after = [chunks[j + 1][1]] if j + 1 < n else []
        jobs = [job for job in pending if job[0] <= j - 3]
        if j == 5:
            jobs += [returned]
        pending = [job for job in pending if job[0] > j - 3]
        mine, others, result = contract(
            table, chunks[j], panels, eps, eps_both, layout, j, result, jobs, after
        )
        received = lax.ppermute(others, "occ", [(1, 0), (2, 3)])
        if j == 0:
            returned = (0, [route(pack_results(table, mine, received, layout, 0))])
            if n < 6:
                pending.append(returned)
        else:
            pending.append((j, [mine, received]))
    result = place(table, result, layout, pending)
    return result.reshape(NB_DEV * block_cols, width)


def solution(mesh):
    in_specs = (P("vir", "occ"), P("occ", "vir"), P("vir"), P("occ"), P(), P())
    out_specs = P("vir", "occ")
    return jax.shard_map(local, mesh=mesh, in_specs=in_specs, out_specs=out_specs, check_vma=False)
```
